32 devices in a mesh: groups: 2 (over x), ent: 16 (over z, y, core).
Axes of the slice: x: 2, y: 2, z: 4, core: 2. Of those that a mesh axis runs over, the one named last changes fastest.
Arguments:
- table: float32 [16384, 400], P(('groups', 'ent')), parts along dimension 0, may hold values from -0.75 to 0.75
- accum: float32 [16384, 400], P(('groups', 'ent')), parts along dimension 0, may hold values from 0.01 to 1
- relations: bfloat16 [8192, 400], P('groups'), parts along dimension 0, may hold values from -0.75 to 0.75
- edges: int32 [16384, 3], P(('groups', 'ent')), parts along dimension 0, may hold values from 0 to 8191, as said below
- negatives: int32 [32], P(('groups', 'ent')), parts along dimension 0, may hold values from 0 to 31
- block_map: int32 [512], P('groups'), parts along dimension 0, may hold values from 0 to 255, as said below
Outputs:
- new_table: float32 [16384, 400], P(('groups', 'ent')), parts along dimension 0
- new_accum: float32 [16384, 400], P(('groups', 'ent')), parts along dimension 0
The draws below stay inside these ranges and needn't reach their ends.
There are 2 independent parts, one for each index of `groups`. The reference program is written for one: setup_inputs(seed, part) draws one part's arguments, and reference() takes and returns one part's arrays. A program takes and returns all parts, laid end to end along the dimension named above; each array names one. Nothing has to cross between parts.
Inputs may be any that keep to these rules, and one draw needn't show every extreme that they name: Column 0 and column 2 hold entity ids, column 1 relation ids below 4096. Among the 1024 head and tail ids of one device's edges, at most 128 have storage rows on any one device (row(e) // 512); in every draw one device receives exactly 128 from every device. `block_map`: A permutation of the blocks.
All inputs are finite; a program needn't handle non-finite values.
Results may differ from the reference program's by a relative error of at most 0.0045.
Values may be sent and summed in bfloat16 or wider, within the bound.
A program may use at most 64 MiB of HBM per device.

```python
import math
import jax
import jax.numpy as jnp
from jax import lax

D = 200
REL = 4096
ENT_DEV = 512
B_DEV = 512
BLK = 32
SPAN = 16
CAP = 128
CH_DEV = 32
ENTITIES = 8192
NBLK = 256
N_ENT = 16


def shared_layout(key):
    shuffled = jax.random.permutation(jax.random.fold_in(key, 5), NBLK).astype(jnp.int32)
    return (shuffled, jnp.argsort(shuffled).astype(jnp.int32))


def draw_block_map(key, part):
    placed, inverse = shared_layout(key)
    return placed


def draw_table(key, part):
    key = jax.random.fold_in(key, 11)
    key_values = jax.random.fold_in(key, 0)
    values = jax.random.uniform(key_values, (ENTITIES, 2 * D), jnp.float32, -0.75, 0.75)
    return values


def device_requests(device_key, hot_owner, inverse):
    total_count = 2 * B_DEV
    slot_count = N_ENT * CAP
    key_weight, key_priority, key_rows, key_order, key_relation = jax.random.split(device_key, 5)
    weight = jax.random.randint(key_weight, (N_ENT,), 0, 4)
    priority = jax.random.randint(key_priority, (slot_count,), 0, 65536)
    slot_owner = jnp.arange(slot_count, dtype=jnp.int32) // CAP
    scores = (jnp.take(weight, slot_owner) * 65536 + priority) * slot_count + jnp.arange(slot_count, dtype=jnp.int32)
    scores = jnp.where(slot_owner == hot_owner, -1, scores)
    chosen_values, picked = lax.top_k(scores, total_count - CAP)
    owners = jnp.concatenate([jnp.full((CAP,), hot_owner, jnp.int32), jnp.take(slot_owner, picked)])
    local_rows = jax.random.randint(key_rows, (total_count,), 0, ENT_DEV)
    stored = owners * ENT_DEV + local_rows
    entity = jnp.take(inverse, stored // BLK) * BLK + stored % BLK
    entity = jnp.take(entity, jax.random.permutation(key_order, total_count))
    relation_ids = jax.random.randint(key_relation, (B_DEV,), 0, REL)
    return jnp.stack([entity[:B_DEV], relation_ids, entity[B_DEV:]], axis=1).astype(jnp.int32)


def draw_edges(key, part):
    placed, inverse = shared_layout(key)
    key = jax.random.fold_in(key, 7)
    key_hot, key_devices = jax.random.split(key)
    hot_owner = jax.random.randint(key_hot, (), 0, N_ENT)
    device_keys = jax.random.split(key_devices, N_ENT)
    stacked = jax.vmap(lambda device_key: device_requests(device_key, hot_owner, inverse))(device_keys)
    return stacked.reshape(B_DEV * N_ENT, 3)


def place_ends(drawn, own_key, least, high):
    dims = drawn.shape
    index_at = [jax.random.randint(jax.random.fold_in(own_key, axis), (), 0, dims[axis]) for axis in range(len(dims))]
    drawn = drawn.at[tuple(index_at)].set(least)
    longest = dims.index(max(dims))
    index_at[longest] = (index_at[longest] + 1) % dims[longest]
    return drawn.at[tuple(index_at)].set(high)


def level_of(rng, shape, cuts, low, high):
    def one(position, parts):
        steps = jax.random.uniform(jax.random.fold_in(jax.random.fold_in(rng, 6), position), (parts,), jnp.float32, low / len(cuts), high / len(cuts))
        return jnp.repeat(jnp.exp(steps), shape[position] // parts).reshape((-1,) + (1,) * (len(shape) - position - 1))

    gain = one(*cuts[0])
    for cut in cuts[1:]:
        gain = gain * one(*cut)
    return gain


def setup_inputs(seed: int = 0, part: int = 0) -> dict:
    keys = jax.random.split(jax.random.key(seed), 7)
    own_keys = jax.random.split(jax.random.fold_in(keys[6], part), 7)
    return {
        "table": draw_table(jax.random.fold_in(jax.random.fold_in(keys[6], part), 71), part),
        "accum": jnp.clip(jnp.exp(math.log(1.0) - 4.6051702 * jax.random.uniform(own_keys[1], (ENTITIES, 2 * D), jnp.float32) ** level_of(own_keys[1], (ENTITIES, 2 * D), ((0, 16),), -0.2, 0.2)), 0.01, 1.0),
        "relations": jnp.clip(jax.random.uniform(own_keys[2], (REL, 2 * D), jnp.float32, -0.75, 0.75), -0.75, 0.75).astype(jnp.bfloat16),
        "edges": draw_edges(jax.random.fold_in(jax.random.fold_in(keys[6], part), 71), part),
        "negatives": place_ends(jax.random.randint(own_keys[4], (N_ENT,), 0, CH_DEV), jax.random.fold_in(own_keys[4], 1), 0, CH_DEV - 1).astype(jnp.int32),
        "block_map": draw_block_map(jax.random.fold_in(jax.random.fold_in(keys[6], part), 71), part),
    }


temper = 2.0
learn_rate = 0.1
epsilon = 1e-10

def storage_rows(entity_ids, block_map):
    return (jnp.take(block_map, entity_ids // BLK) * BLK + entity_ids % BLK).astype(jnp.int32)

def complex_product(left, right):
    left_re, left_im = (left[:, :D], left[:, D:])
    right_re, right_im = (right[:, :D], right[:, D:])
    return jnp.concatenate([left_re * right_re - left_im * right_im, left_re * right_im + left_im * right_re], axis=1)

def conjugate_product(grads, right):
    grad_re, grad_im = (grads[:, :D], grads[:, D:])
    right_re, right_im = (right[:, :D], right[:, D:])
    return jnp.concatenate([grad_re * right_re + grad_im * right_im, grad_im * right_re - grad_re * right_im], axis=1)

def reference(table, accum, relations, edges, negatives, block_map):
    table_bf = table.astype(jnp.bfloat16)
    head_index = storage_rows(edges[:, 0], block_map)
    tail_index = storage_rows(edges[:, 2], block_map)
    head_rows = jnp.take(table_bf, head_index, axis=0).astype(jnp.float32)
    tail_rows = jnp.take(table_bf, tail_index, axis=0).astype(jnp.float32)
    relation_rows = jnp.take(relations, edges[:, 1], axis=0).astype(jnp.float32)
    starts = jnp.arange(N_ENT, dtype=jnp.int32) * ENT_DEV + negatives.astype(jnp.int32) * SPAN
    negative_index = (starts[:, None] + jnp.arange(SPAN, dtype=jnp.int32)[None, :]).reshape(-1)
    negs = jnp.take(table_bf, negative_index, axis=0)
    queries = complex_product(head_rows, relation_rows)
    queries_bf = queries.astype(jnp.bfloat16)
    positive = lax.optimization_barrier(jnp.sum(queries * tail_rows, axis=1))
    negative = jnp.dot(queries_bf, negs.T, preferred_element_type=jnp.float32)
    tempered = jnp.exp(temper * negative)
    weights = tempered / lax.optimization_barrier(jnp.sum(tempered, axis=1, keepdims=True))
    grad_positive = -(1.0 - jax.nn.sigmoid(positive))
    grad_negative = (weights * jax.nn.sigmoid(negative)).astype(jnp.bfloat16)
    grad_query = grad_positive[:, None] * tail_rows + jnp.dot(grad_negative, negs, preferred_element_type=jnp.float32)
    grad_head = conjugate_product(grad_query, relation_rows)
    grad_tail = grad_positive[:, None] * queries
    grad_negs = jnp.dot(grad_negative.T, queries_bf, preferred_element_type=jnp.float32)
    gradient = jnp.zeros(table.shape, jnp.float32)
    gradient = gradient.at[head_index].add(grad_head)
    gradient = gradient.at[tail_index].add(grad_tail)
    gradient = gradient.at[negative_index].add(grad_negs)
    new_accum = accum + gradient * gradient
    new_table = table - learn_rate * gradient / (jnp.sqrt(new_accum) + epsilon)
    return (new_table, new_accum)
```

```python
import functools

import jax
import jax.numpy as jnp
from jax import lax
from jax.experimental import pallas as pl
from jax.experimental.pallas import tpu as pltpu
from jax.sharding import PartitionSpec as P

BLK = 32
SPAN = 16
W = 256

temper = 2.0
learn_rate = 0.1
epsilon = 1e-10

F32 = jnp.float32
BF16 = jnp.bfloat16


def dot(a, b):
    return jnp.dot(a, b, preferred_element_type=F32)


def iota(shape, dim):
    return lax.broadcasted_iota(jnp.int32, shape, dim).astype(F32)


def onehot(mask):
    return jnp.where(mask, 1.0, 0.0).astype(BF16)


def sigmoid(x):
    return 1.0 / (1.0 + jnp.exp(-x))


def kernel(
    n,
    snake,
    table,
    edges,
    negative,
    block_map,
    rel_hbm,
    out,
    ag,
    agp,
    rs,
    gath,
    rel,
    relg,
    ids_own,
    ids_part,
    idcol,
    grads,
    grads_part,
    negrow,
    negcol,
    negpart,
    negsend,
    negrecv,
    part,
    partneg,
    ag_send,
    ag_recv,
    agp_send,
    agp_recv,
    rs_send,
    rs_recv,
    x_send,
    x_recv,
    rel_sem,
):
    feat, rows = table.shape
    dims = feat // 2
    edge_count = edges.shape[1]
    echunks = edge_count // W
    gchunks = 2 * echunks
    nneg = 2 * n * SPAN
    nchunks = nneg // W
    nblk = block_map.shape[1]
    rel_count = rel_hbm.shape[1]
    ag_rows = feat + 16
    rs_rows = feat + 32
    cut = 208
    ag_subs = ((0, cut), (cut, ag_rows - cut))
    rs_subs = ((0, cut), (cut, rs_rows - cut))

    me = lax.axis_index("ent")
    core = lax.rem(me, 2)
    chip = me // 2
    if snake:
        z, y = chip // 2, lax.rem(chip, 2)
        pos = (1 - y) * z + y * (n - 1 - z)
    else:
        pos = chip

    def chip_at(p):
        p = lax.rem(p + 2 * n, n)
        if not snake:
            return p
        f = p // (n // 2)
        return (1 - f) * 2 * p + f * (2 * (n - 1 - p) + 1)

    partner = 2 * chip + 1 - core
    nxt = (2 * chip_at(pos + 1) + core, 2 * chip_at(pos - 1) + core)

    rel_copy = pltpu.make_async_copy(rel_hbm, rel, rel_sem)
    rel_copy.start()

    barrier = pltpu.get_barrier_semaphore()
    for other in (nxt[0], nxt[1], partner):
        pl.semaphore_signal(
            barrier, inc=1, device_id={"ent": other}, device_id_type=pl.DeviceIdType.MESH
        )

    def remote(src, dst, send, recv, to):
        return pltpu.make_async_remote_copy(
            src_ref=src,
            dst_ref=dst,
            send_sem=send,
            recv_sem=recv,
            device_id={"ent": to},
            device_id_type=pl.DeviceIdType.MESH,
        )

    def ag_copy(k, d, s):
        at, size = ag_subs[s]
        return remote(
            ag.at[k - 1, d, pl.ds(at, size)],
            ag.at[k, d, pl.ds(at, size)],
            ag_send.at[k, d, s],
            ag_recv.at[k, d, s],
            nxt[d],
        )

    def agp_copy(k, d):
        return remote(
            ag.at[k, d, pl.ds(0, ag_rows)],
            agp.at[k, d],
            agp_send.at[k, d],
            agp_recv.at[k, d],
            partner,
        )

    def rs_copy(k, d, s):
        at, size = rs_subs[s]
        return remote(
            ag.at[k, d, pl.ds(at, size)],
            rs.at[k, d, pl.ds(at, size)],
            rs_send.at[k, d, s],
            rs_recv.at[k, d, s],
            nxt[d],
        )

    for d in range(2):
        ag[0, d, 0:feat, :] = table[:, d * W : (d + 1) * W].astype(BF16)
        ag[0, d, feat:ag_rows, :] = jnp.full((16, W), negative[0], jnp.int32).astype(F32).astype(BF16)
    pl.semaphore_wait(barrier, 3)
    for s in range(2):
        for d in range(2):
            ag_copy(1, d, s).start()
    for d in range(2):
        agp_copy(0, d).start()

    ends = jnp.concatenate([edges[0:1, :], edges[2:3, :]], axis=1)
    mapped = block_map[...]
    parts = jnp.concatenate(
        [
            jnp.broadcast_to((mapped >> 5).astype(F32), (8, nblk)),
            jnp.broadcast_to((mapped & 31).astype(F32), (8, nblk)),
        ],
        axis=0,
    ).astype(BF16)
    for c in range(gchunks):
        cols = slice(c * W, (c + 1) * W)
        of = ends[:, cols]
        found = dot(parts, onehot(iota((nblk, W), 0) == (of >> 5).astype(F32)))
        ids_own[:, cols] = (found[0:8] * 32.0 + found[8:16]) * float(BLK) + (of & 31).astype(F32)
    ids_copy = remote(ids_own, ids_part, x_send.at[0], x_recv.at[0], partner)
    ids_copy.start()

    sub_iota = iota((W, W), 0)
    lane_iota = iota((1, W), 1)

    def set_columns(held, first):
        for c in range(gchunks):
            turned = jnp.transpose(held[:, c * W : (c + 1) * W])
            idcol[first + c] = jnp.broadcast_to(turned[:, 0:1], (W, 128))

    set_columns(ids_own, 0)

    rel_copy.wait()
    relg[...] = jnp.zeros_like(relg)

    @pl.loop(0, rel_count // W)
    def _(kk):
        cols = pl.ds(pl.multiple_of(kk * W, W), W)
        for c in range(echunks):
            local = edges[1:2, c * W : (c + 1) * W].astype(F32) - (kk * W).astype(F32)
            relg[c] += dot(rel[:, cols], onehot(sub_iota == local))

    gath[...] = jnp.zeros_like(gath)

    def take(buf, k, on_core):
        for d in range(2):
            at_chip = chip_at(pos - k if d == 0 else pos + k)
            base = ((2 * at_chip + on_core) * rows + d * W).astype(F32)
            first = (on_core * (n * SPAN) + at_chip * SPAN).astype(F32)
            value = buf[k, d, feat:ag_rows, :].astype(F32)[0:1, :]
            slab = buf.at[k, d, pl.ds(0, feat)]
            for c in range(gchunks):
                local = ids_own[0:1, c * W : (c + 1) * W] - base
                gath[c] += dot(slab[...], onehot(sub_iota == local))
            for c in range(nchunks):
                place = lane_iota + (float(c * W) - first)
                local = jnp.where(
                    (place >= 0.0) & (place < float(SPAN)),
                    value * float(SPAN) + place - float(d * W),
                    -1.0,
                )
                gath[gchunks + c] += dot(slab[...], onehot(sub_iota == local))

    take(ag, 0, core)

    @pl.loop(1, n)
    def _(k):
        for s in range(2):
            for d in range(2):
                ag_copy(k, d, s).wait_recv()

                @pl.when(k < n - 1)
                def _():
                    ag_copy(k + 1, d, s).start()

        for d in range(2):
            agp_copy(k, d).start()
        take(ag, k, core)
        for d in range(2):
            agp_copy(k - 1, d).wait_recv()
        take(agp, k - 1, 1 - core)

    for d in range(2):
        agp_copy(n - 1, d).wait_recv()
    take(agp, n - 1, 1 - core)

    @pl.loop(0, n)
    def _(k):
        for d in range(2):
            agp_copy(k, d).wait_send()

            @pl.when(k > 0)
            def _():
                for s in range(2):
                    ag_copy(k, d, s).wait_send()

    for c in range(nchunks):
        held = gath[gchunks + c]
        negcol[:, c * W : (c + 1) * W] = held.astype(BF16)
        negrow[c * W : (c + 1) * W, :] = jnp.transpose(held).astype(BF16)
    negpart[...] = jnp.zeros_like(negpart)
    for c in range(echunks):
        head, tail, rl = gath[c], gath[echunks + c], relg[c]
        h_re, h_im, r_re, r_im = head[:dims], head[dims:], rl[:dims], rl[dims:]
        queries = jnp.concatenate([h_re * r_re - h_im * r_im, h_re * r_im + h_im * r_re], axis=0)
        queries_bf = queries.astype(BF16)
        positive = jnp.sum(queries * tail, axis=0, keepdims=True)
        score = dot(negrow[...], queries_bf)
        tempered = jnp.exp(temper * score)
        weights = tempered / jnp.sum(tempered, axis=0, keepdims=True)
        grad_positive = -(1.0 - sigmoid(positive))
        grad_negative = (weights * sigmoid(score)).astype(BF16)
        grad_query = grad_positive * tail + dot(negcol[...], grad_negative)
        g_re, g_im = grad_query[:dims], grad_query[dims:]
        grads[c] = jnp.concatenate(
            [g_re * r_re + g_im * r_im, g_im * r_re - g_re * r_im], axis=0
        ).astype(BF16)
        grads[echunks + c] = (grad_positive * queries).astype(BF16)
        negpart[:, 0:feat] += lax.dot_general(
            grad_negative, queries_bf, (((1,), (1,)), ((), ())), preferred_element_type=F32
        )
    half = n * SPAN
    grads_copy = remote(grads, grads_part, x_send.at[1], x_recv.at[1], partner)
    grads_copy.start()
    negsend[...] = negpart[pl.ds(pl.multiple_of((1 - core) * half, half), half), :].astype(BF16)
    neg_copy = remote(negsend, negrecv, x_send.at[2], x_recv.at[2], partner)
    neg_copy.start()
    ids_copy.wait()
    set_columns(ids_part, gchunks)

    lanes = iota((W, 128), 1)

    def gradient_part(k, d, held, first, fresh):
        at_chip = chip_at(pos - 1 - k if d == 0 else pos + 1 + k)
        base = ((2 * at_chip + core) * rows + d * W).astype(F32)
        total = None
        for c in range(gchunks):
            col = idcol[first + c] - base
            mask = jnp.concatenate([onehot(col == lanes), onehot(col == lanes + 128.0)], axis=1)
            one = dot(held[c], mask)
            total = one if total is None else total + one
        if fresh:
            part[d] = total
        else:
            part[d] += total

    def negative_part(k, d):
        at_chip = chip_at(pos - 1 - k if d == 0 else pos + 1 + k)
        own = negpart[pl.ds(pl.multiple_of(core * half + at_chip * SPAN, SPAN), SPAN), d * W : (d + 1) * W]
        other = negrecv[pl.ds(pl.multiple_of(at_chip * SPAN, SPAN), SPAN), d * W : (d + 1) * W]
        partneg[d] = own + other.astype(F32)

    def send_out(k, d, s, arrived):
        at, size = rs_subs[s]
        if s == 0:
            value = part[d, 0:cut]
            if arrived:
                value = value + rs[k - 1, d, 0:cut].astype(F32)
            ag[k, d, 0:cut] = value.astype(BF16)
        else:
            value = part[d, cut:feat]
            neg = partneg[d]
            if arrived:
                value = value + rs[k - 1, d, cut:feat].astype(F32)
                neg = neg + (
                    rs[k - 1, d, feat : feat + 16].astype(F32)
                    + rs[k - 1, d, feat + 16 : feat + 32].astype(F32)
                )
            ag[k, d, cut:feat] = value.astype(BF16)
            high = neg.astype(BF16)
            ag[k, d, feat : feat + 16] = high
            ag[k, d, feat + 16 : feat + 32] = (neg - high.astype(F32)).astype(BF16)
        rs_copy(k, d, s).start()

    for d in range(2):
        gradient_part(0, d, grads, 0, True)
    grads_copy.wait()
    for d in range(2):
        gradient_part(0, d, grads_part, gchunks, False)
    neg_copy.wait()
    for d in range(2):
        negative_part(0, d)
    for s in range(2):
        for d in range(2):
            send_out(0, d, s, False)

    def both(k):
        for d in range(2):
            gradient_part(k, d, grads, 0, True)
            gradient_part(k, d, grads_part, gchunks, False)
            negative_part(k, d)

    @pl.loop(1, n - 1)
    def _(k):
        both(k)
        for s in range(2):
            for d in range(2):
                rs_copy(k - 1, d, s).wait_recv()
                send_out(k, d, s, True)

    both(n - 1)
    last = n - 2
    spot = jnp.full((1, rows), negative[0], jnp.int32).astype(F32) * float(SPAN)
    span_iota = iota((SPAN, rows), 0)
    row_iota = iota((1, rows), 1)
    mask = jnp.where(row_iota - spot == span_iota, 1.0, 0.0)
    mask = jnp.concatenate([mask, mask], axis=0).astype(BF16)
    for d in range(2):
        for s in range(2):
            rs_copy(last, d, s).wait_recv()
        out[:, d * W : (d + 1) * W] = part[d] + rs[last, d, 0:feat].astype(F32)
    for d in range(2):
        neg = partneg[d] + (
            rs[last, d, feat : feat + 16].astype(F32) + rs[last, d, feat + 16 : feat + 32].astype(F32)
        )
        high = neg.astype(BF16).astype(F32)
        pair = jnp.concatenate([high, neg - high], axis=0).astype(BF16)
        spread = lax.dot_general(
            pair, mask, (((0,), (0,)), ((), ())), preferred_element_type=F32
        )
        size = min(feat - d * W, W)
        out[d * W : d * W + size, :] += spread[:size]

    @pl.loop(0, n - 1)
    def _(k):
        for d in range(2):
            for s in range(2):
                rs_copy(k, d, s).wait_send()


def gradient_of(table, edges, negatives, block_map, relations, n):
    feat, rows = table.shape
    edge_count = edges.shape[1]
    gchunks = 2 * edge_count // W
    nneg = 2 * n * SPAN
    dma = pltpu.SemaphoreType.DMA
    vmem = pl.BlockSpec(memory_space=pltpu.VMEM)
    return pl.pallas_call(
        functools.partial(kernel, n, n == 8),
        out_shape=jax.ShapeDtypeStruct((feat, rows), F32),
        in_specs=[
            vmem,
            vmem,
            pl.BlockSpec(memory_space=pltpu.SMEM),
            vmem,
            pl.BlockSpec(memory_space=pl.ANY),
        ],
        out_specs=vmem,
        scratch_shapes=[
            pltpu.VMEM((n, 2, feat + 32, W), BF16),
            pltpu.VMEM((n, 2, feat + 16, W), BF16),
            pltpu.VMEM((n - 1, 2, feat + 32, W), BF16),
            pltpu.VMEM((gchunks + nneg // W, feat, W), F32),
            pltpu.VMEM(relations.shape, BF16),
            pltpu.VMEM((edge_count // W, feat, W), F32),
            pltpu.VMEM((8, 2 * edge_count), F32),
            pltpu.VMEM((8, 2 * edge_count), F32),
            pltpu.VMEM((2 * gchunks, W, 128), F32),
            pltpu.VMEM((gchunks, feat, W), BF16),
            pltpu.VMEM((gchunks, feat, W), BF16),
            pltpu.VMEM((nneg, feat), BF16),
            pltpu.VMEM((feat, nneg), BF16),
            pltpu.VMEM((nneg, 2 * W), F32),
            pltpu.VMEM((nneg // 2, 2 * W), BF16),
            pltpu.VMEM((nneg // 2, 2 * W), BF16),
            pltpu.VMEM((2, feat, W), F32),
            pltpu.VMEM((2, SPAN, W), F32),
            dma((n, 2, 2)),
            dma((n, 2, 2)),
            dma((n, 2)),
            dma((n, 2)),
            dma((n - 1, 2, 2)),
            dma((n - 1, 2, 2)),
            dma((3,)),
            dma((3,)),
            dma,
        ],
        compiler_params=pltpu.CompilerParams(
            collective_id=0, has_side_effects=True, vmem_limit_bytes=60 * 2**20
        ),
        name="complex_step",
    )(table, edges, negatives, block_map, relations)


def on_device(table, accum, relations, edges, negatives, block_map):
    n = lax.axis_size("ent") // 2
    gradient = gradient_of(
        table.T, edges.T, negatives, block_map.reshape(1, -1), relations.T, n
    ).T
    new_accum = accum + gradient * gradient
    new_table = table - learn_rate * gradient / (jnp.sqrt(new_accum) + epsilon)
    return (new_table, new_accum)


def solution(mesh):
    placed = (
        P(("groups", "ent"), None),
        P(("groups", "ent"), None),
        P("groups", None),
        P(("groups", "ent"), None),
        P(("groups", "ent")),
        P("groups"),
    )
    return jax.shard_map(
        on_device,
        mesh=mesh,
        in_specs=placed,
        out_specs=(P(("groups", "ent"), None), P(("groups", "ent"), None)),
        check_vma=False,
    )
```

```python
import functools

import jax
import jax.numpy as jnp
from jax import lax
from jax.experimental import pallas as pl
from jax.experimental.pallas import tpu as pltpu
from jax.sharding import PartitionSpec as P

BLK = 32
SPAN = 16
AG_PIECES = 4
RS_PIECES = 3
W = 256

temper = 2.0
learn_rate = 0.1
epsilon = 1e-10

F32 = jnp.float32
BF16 = jnp.bfloat16


def pieces(rows, count):
    tiles = rows // 16
    ends = [16 * (tiles * i // count) for i in range(count + 1)]
    return tuple((at, end - at) for at, end in zip(ends[:-1], ends[1:]))


def dot(a, b):
    return jnp.dot(a, b, preferred_element_type=F32)


def iota(shape, dim):
    return lax.broadcasted_iota(jnp.int32, shape, dim).astype(F32)


def onehot(mask):
    return jnp.where(mask, 1.0, 0.0).astype(BF16)


def sigmoid(x):
    return 1.0 / (1.0 + jnp.exp(-x))


def kernel(
    n,
    snake,
    table_hbm,
    edges,
    negative,
    block_map,
    rel_hbm,
    out,
    table,
    ag,
    agp,
    nid,
    nidp,
    rs,
    gath,
    rel,
    relg,
    ids_own,
    ids_part,
    idcol,
    grads,
    grads_part,
    negrow,
    negcol,
    negpart,
    negsend,
    negrecv,
    part,
    partneg,
    ag_send,
    ag_recv,
    agp_send,
    agp_recv,
    nid_send,
    nid_recv,
    nidp_send,
    nidp_recv,
    rs_send,
    rs_recv,
    x_send,
    x_recv,
    rel_sem,
    table_sem,
):
    feat, rows = table_hbm.shape
    dims = feat // 2
    edge_count = edges.shape[1]
    echunks = edge_count // W
    gchunks = 2 * echunks
    nneg = 2 * n * SPAN
    nchunks = nneg // W
    nblk = block_map.shape[1]
    rel_count = rel_hbm.shape[1]
    ag_rows = feat
    rs_rows = feat + 32
    ag_subs = pieces(ag_rows, AG_PIECES)
    rs_subs = pieces(rs_rows, RS_PIECES)

    me = lax.axis_index("ent")
    core = lax.rem(me, 2)
    chip = me // 2
    if snake:
        z, y = chip // 2, lax.rem(chip, 2)
        pos = (1 - y) * z + y * (n - 1 - z)
    else:
        pos = chip

    def chip_at(p):
        p = lax.rem(p + 2 * n, n)
        if not snake:
            return p
        f = p // (n // 2)
        return (1 - f) * 2 * p + f * (2 * (n - 1 - p) + 1)

    partner = 2 * chip + 1 - core
    nxt = (2 * chip_at(pos + 1) + core, 2 * chip_at(pos - 1) + core)

    halves = [slice(d * W, (d + 1) * W) for d in range(2)]
    table_copies = [
        pltpu.make_async_copy(table_hbm.at[:, cols], table.at[:, cols], table_sem.at[d])
        for d, cols in enumerate(halves)
    ]
    for copy in table_copies:
        copy.start()
    rel_copy = pltpu.make_async_copy(rel_hbm, rel, rel_sem)
    rel_copy.start()

    barrier = pltpu.get_barrier_semaphore()
    for other in (nxt[0], nxt[1], partner):
        pl.semaphore_signal(
            barrier, inc=1, device_id={"ent": other}, device_id_type=pl.DeviceIdType.MESH
        )

    def remote(src, dst, send, recv, to):
        return pltpu.make_async_remote_copy(
            src_ref=src,
            dst_ref=dst,
            send_sem=send,
            recv_sem=recv,
            device_id={"ent": to},
            device_id_type=pl.DeviceIdType.MESH,
        )

    def ag_copy(k, d, s):
        at, size = ag_subs[s]
        return remote(
            ag.at[k - 1, d, pl.ds(at, size)],
            ag.at[k, d, pl.ds(at, size)],
            ag_send.at[k, d, s],
            ag_recv.at[k, d, s],
            nxt[d],
        )

    def agp_copy(k, d):
        return remote(
            ag.at[k, d, pl.ds(0, ag_rows)],
            agp.at[k, d],
            agp_send.at[k, d],
            agp_recv.at[k, d],
            partner,
        )

    def nid_copy(k, d):
        return remote(
            nid.at[k - 1, d], nid.at[k, d], nid_send.at[k, d], nid_recv.at[k, d], nxt[d]
        )

    def nidp_copy(k, d):
        return remote(
            nid.at[k, d], nidp.at[k, d], nidp_send.at[k, d], nidp_recv.at[k, d], partner
        )

    def rs_copy(k, d, s):
        at, size = rs_subs[s]
        return remote(
            ag.at[k, d, pl.ds(at, size)],
            rs.at[k, d, pl.ds(at, size)],
            rs_send.at[k, d, s],
            rs_recv.at[k, d, s],
            nxt[d],
        )

    for d in range(2):
        table_copies[d].wait()
        ag[0, d, 0:feat, :] = table[:, d * W : (d + 1) * W].astype(BF16)
        nid[0, d] = jnp.full((1, 128), negative[0], jnp.int32).astype(F32)
    pl.semaphore_wait(barrier, 3)
    for d in range(2):
        nid_copy(1, d).start()
    for s in range(AG_PIECES):
        for d in range(2):
            ag_copy(1, d, s).start()
    for d in range(2):
        nidp_copy(0, d).start()
        agp_copy(0, d).start()

    ends = jnp.concatenate([edges[0:1, :], edges[2:3, :]], axis=1)
    mapped = block_map[...]
    parts = jnp.concatenate(
        [
            jnp.broadcast_to((mapped >> 5).astype(F32), (8, nblk)),
            jnp.broadcast_to((mapped & 31).astype(F32), (8, nblk)),
        ],
        axis=0,
    ).astype(BF16)
    for c in range(gchunks):
        cols = slice(c * W, (c + 1) * W)
        of = ends[:, cols]
        found = dot(parts, onehot(iota((nblk, W), 0) == (of >> 5).astype(F32)))
        ids_own[:, cols] = (found[0:8] * 32.0 + found[8:16]) * float(BLK) + (of & 31).astype(F32)
    ids_copy = remote(ids_own, ids_part, x_send.at[0], x_recv.at[0], partner)
    ids_copy.start()

    sub_iota = iota((W, W), 0)
    lane_iota = iota((1, W), 1)

    def set_columns(held, first):
        for c in range(gchunks):
            turned = jnp.transpose(held[:, c * W : (c + 1) * W])
            idcol[first + c] = jnp.broadcast_to(turned[:, 0:1], (W, 128))

    set_columns(ids_own, 0)

    rel_copy.wait()
    relg[...] = jnp.zeros_like(relg)

    @pl.loop(0, rel_count // W)
    def _(kk):
        cols = pl.ds(pl.multiple_of(kk * W, W), W)
        for c in range(echunks):
            local = edges[1:2, c * W : (c + 1) * W].astype(F32) - (kk * W).astype(F32)
            relg[c] += dot(rel[:, cols], onehot(sub_iota == local))

    gath[...] = jnp.zeros_like(gath)

    def take(buf, spans, k, on_core, dirs=(0, 1)):
        for d in dirs:
            at_chip = chip_at(pos - k if d == 0 else pos + k)
            base = ((2 * at_chip + on_core) * rows + d * W).astype(F32)
            first = (on_core * (n * SPAN) + at_chip * SPAN).astype(F32)
            value = jnp.concatenate([spans[k, d]] * (W // 128), axis=1)
            slab = buf.at[k, d, pl.ds(0, feat)]
            for c in range(gchunks):
                local = ids_own[0:1, c * W : (c + 1) * W] - base
                gath[c] += dot(slab[...], onehot(sub_iota == local))
            for c in range(nchunks):
                place = lane_iota + (float(c * W) - first)
                local = jnp.where(
                    (place >= 0.0) & (place < float(SPAN)),
                    value * float(SPAN) + place - float(d * W),
                    -1.0,
                )
                gath[gchunks + c] += dot(slab[...], onehot(sub_iota == local))

    take(ag, nid, 0, core)

    @pl.loop(1, n)
    def _(k):
        for d in range(2):
            nid_copy(k, d).wait_recv()

            @pl.when(k < n - 1)
            def _():
                nid_copy(k + 1, d).start()

            nidp_copy(k, d).start()
        for s in range(AG_PIECES):
            for d in range(2):
                ag_copy(k, d, s).wait_recv()

                @pl.when(k < n - 1)
                def _():
                    ag_copy(k + 1, d, s).start()

            if s < 2:
                nidp_copy(k - 1, s).wait_recv()
                agp_copy(k - 1, s).wait_recv()
                take(agp, nidp, k - 1, 1 - core, (s,))
        for d in range(2):
            agp_copy(k, d).start()
        take(ag, nid, k, core)

    for d in range(2):
        nidp_copy(n - 1, d).wait_recv()
        agp_copy(n - 1, d).wait_recv()
    take(agp, nidp, n - 1, 1 - core)

    @pl.loop(0, n)
    def _(k):
        for d in range(2):
            agp_copy(k, d).wait_send()
            nidp_copy(k, d).wait_send()

            @pl.when(k > 0)
            def _():
                nid_copy(k, d).wait_send()
                for s in range(AG_PIECES):
                    ag_copy(k, d, s).wait_send()

    def grads_copy(c):
        return remote(grads.at[c], grads_part.at[c], x_send.at[2 + c], x_recv.at[2 + c], partner)

    for c in range(nchunks):
        held = gath[gchunks + c]
        negcol[:, c * W : (c + 1) * W] = held.astype(BF16)
        negrow[c * W : (c + 1) * W, :] = jnp.transpose(held).astype(BF16)
    negpart[...] = jnp.zeros_like(negpart)
    for c in range(echunks):
        head, tail, rl = gath[c], gath[echunks + c], relg[c]
        h_re, h_im, r_re, r_im = head[:dims], head[dims:], rl[:dims], rl[dims:]
        queries = jnp.concatenate([h_re * r_re - h_im * r_im, h_re * r_im + h_im * r_re], axis=0)
        queries_bf = queries.astype(BF16)
        positive = jnp.sum(queries * tail, axis=0, keepdims=True)
        score = dot(negrow[...], queries_bf)
        tempered = jnp.exp(temper * score)
        weights = tempered / jnp.sum(tempered, axis=0, keepdims=True)
        grad_positive = -(1.0 - sigmoid(positive))
        grad_negative = (weights * sigmoid(score)).astype(BF16)
        grad_query = grad_positive * tail + dot(negcol[...], grad_negative)
        g_re, g_im = grad_query[:dims], grad_query[dims:]
        grads[c] = jnp.concatenate(
            [g_re * r_re + g_im * r_im, g_im * r_re - g_re * r_im], axis=0
        ).astype(BF16)
        grads[echunks + c] = (grad_positive * queries).astype(BF16)
        grads_copy(c).start()
        grads_copy(echunks + c).start()
        negpart[:, 0:feat] += lax.dot_general(
            grad_negative, queries_bf, (((1,), (1,)), ((), ())), preferred_element_type=F32
        )
    half = n * SPAN
    negsend[...] = negpart[pl.ds(pl.multiple_of((1 - core) * half, half), half), :].astype(BF16)
    neg_copy = remote(negsend, negrecv, x_send.at[1], x_recv.at[1], partner)
    neg_copy.start()
    ids_copy.wait()
    set_columns(ids_part, gchunks)

    lanes = iota((W, 128), 1)

    def gradient_part(k, d, held, first, fresh):
        at_chip = chip_at(pos - 1 - k if d == 0 else pos + 1 + k)
        base = ((2 * at_chip + core) * rows + d * W).astype(F32)
        total = None
        for c in range(gchunks):
            col = idcol[first + c] - base
            mask = jnp.concatenate([onehot(col == lanes), onehot(col == lanes + 128.0)], axis=1)
            one = dot(held[c], mask)
            total = one if total is None else total + one
        if fresh:
            part[d] = total
        else:
            part[d] += total

    def negative_part(k, d):
        at_chip = chip_at(pos - 1 - k if d == 0 else pos + 1 + k)
        own = negpart[pl.ds(pl.multiple_of(core * half + at_chip * SPAN, SPAN), SPAN), d * W : (d + 1) * W]
        other = negrecv[pl.ds(pl.multiple_of(at_chip * SPAN, SPAN), SPAN), d * W : (d + 1) * W]
        partneg[d] = own + other.astype(F32)

    def send_out(k, d, s, arrived):
        at, size = rs_subs[s]
        end = min(at + size, feat)
        value = part[d, at:end]
        if arrived:
            value = value + rs[k - 1, d, at:end].astype(F32)
        ag[k, d, at:end] = value.astype(BF16)
        if at + size > feat:
            neg = partneg[d]
            if arrived:
                neg = neg + (
                    rs[k - 1, d, feat : feat + 16].astype(F32)
                    + rs[k - 1, d, feat + 16 : feat + 32].astype(F32)
                )
            high = neg.astype(BF16)
            ag[k, d, feat : feat + 16] = high
            ag[k, d, feat + 16 : feat + 32] = (neg - high.astype(F32)).astype(BF16)
        rs_copy(k, d, s).start()

    for d in range(2):
        gradient_part(0, d, grads, 0, True)
    for c in range(gchunks):
        grads_copy(c).wait()
    for d in range(2):
        gradient_part(0, d, grads_part, gchunks, False)
    neg_copy.wait()
    for d in range(2):
        negative_part(0, d)
    for s in range(RS_PIECES):
        for d in range(2):
            send_out(0, d, s, False)

    def both(k):
        for d in range(2):
            gradient_part(k, d, grads, 0, True)
            gradient_part(k, d, grads_part, gchunks, False)
            negative_part(k, d)

    @pl.loop(1, n - 1)
    def _(k):
        both(k)
        for s in range(RS_PIECES):
            for d in range(2):
                rs_copy(k - 1, d, s).wait_recv()
                send_out(k, d, s, True)

    both(n - 1)
    last = n - 2
    spot = jnp.full((1, rows), negative[0], jnp.int32).astype(F32) * float(SPAN)
    span_iota = iota((SPAN, rows), 0)
    row_iota = iota((1, rows), 1)
    mask = jnp.where(row_iota - spot == span_iota, 1.0, 0.0)
    mask = jnp.concatenate([mask, mask], axis=0).astype(BF16)
    for d in range(2):
        for s in range(RS_PIECES):
            rs_copy(last, d, s).wait_recv()
        out[:, d * W : (d + 1) * W] = part[d] + rs[last, d, 0:feat].astype(F32)
    for d in range(2):
        neg = partneg[d] + (
            rs[last, d, feat : feat + 16].astype(F32) + rs[last, d, feat + 16 : feat + 32].astype(F32)
        )
        high = neg.astype(BF16).astype(F32)
        pair = jnp.concatenate([high, neg - high], axis=0).astype(BF16)
        spread = lax.dot_general(
            pair, mask, (((0,), (0,)), ((), ())), preferred_element_type=F32
        )
        size = min(feat - d * W, W)
        out[d * W : d * W + size, :] += spread[:size]

    @pl.loop(0, n - 1)
    def _(k):
        for d in range(2):
            for s in range(RS_PIECES):
                rs_copy(k, d, s).wait_send()


def gradient_of(table, edges, negatives, block_map, relations, n):
    feat, rows = table.shape
    edge_count = edges.shape[1]
    gchunks = 2 * edge_count // W
    nneg = 2 * n * SPAN
    dma = pltpu.SemaphoreType.DMA
    vmem = pl.BlockSpec(memory_space=pltpu.VMEM)
    return pl.pallas_call(
        functools.partial(kernel, n, n == 8),
        out_shape=jax.ShapeDtypeStruct((feat, rows), F32),
        in_specs=[
            pl.BlockSpec(memory_space=pl.ANY),
            vmem,
            pl.BlockSpec(memory_space=pltpu.SMEM),
            vmem,
            pl.BlockSpec(memory_space=pl.ANY),
        ],
        out_specs=vmem,
        scratch_shapes=[
            pltpu.VMEM((feat, rows), F32),
            pltpu.VMEM((n, 2, feat + 32, W), BF16),
            pltpu.VMEM((n, 2, feat, W), BF16),
            pltpu.VMEM((n, 2, 1, 128), F32),
            pltpu.VMEM((n, 2, 1, 128), F32),
            pltpu.VMEM((n - 1, 2, feat + 32, W), BF16),
            pltpu.VMEM((gchunks + nneg // W, feat, W), F32),
            pltpu.VMEM(relations.shape, BF16),
            pltpu.VMEM((edge_count // W, feat, W), F32),
            pltpu.VMEM((8, 2 * edge_count), F32),
            pltpu.VMEM((8, 2 * edge_count), F32),
            pltpu.VMEM((2 * gchunks, W, 128), F32),
            pltpu.VMEM((gchunks, feat, W), BF16),
            pltpu.VMEM((gchunks, feat, W), BF16),
            pltpu.VMEM((nneg, feat), BF16),
            pltpu.VMEM((feat, nneg), BF16),
            pltpu.VMEM((nneg, 2 * W), F32),
            pltpu.VMEM((nneg // 2, 2 * W), BF16),
            pltpu.VMEM((nneg // 2, 2 * W), BF16),
            pltpu.VMEM((2, feat, W), F32),
            pltpu.VMEM((2, SPAN, W), F32),
            dma((n, 2, AG_PIECES)),
            dma((n, 2, AG_PIECES)),
            dma((n, 2)),
            dma((n, 2)),
            dma((n, 2)),
            dma((n, 2)),
            dma((n, 2)),
            dma((n, 2)),
            dma((n - 1, 2, RS_PIECES)),
            dma((n - 1, 2, RS_PIECES)),
            dma((2 + gchunks,)),
            dma((2 + gchunks,)),
            dma,
            dma((2,)),
        ],
        compiler_params=pltpu.CompilerParams(
            collective_id=0, has_side_effects=True, vmem_limit_bytes=60 * 2**20
        ),
        name="complex_step",
    )(table, edges, negatives, block_map, relations)


def on_device(table, accum, relations, edges, negatives, block_map):
    n = lax.axis_size("ent") // 2
    gradient = gradient_of(
        table.T, edges.T, negatives, block_map.reshape(1, -1), relations.T, n
    ).T
    new_accum = accum + gradient * gradient
    new_table = table - learn_rate * gradient / (jnp.sqrt(new_accum) + epsilon)
    return (new_table, new_accum)


def solution(mesh):
    placed = (
        P(("groups", "ent"), None),
        P(("groups", "ent"), None),
        P("groups", None),
        P(("groups", "ent"), None),
        P(("groups", "ent")),
        P("groups"),
    )
    return jax.shard_map(
        on_device,
        mesh=mesh,
        in_specs=placed,
        out_specs=(P(("groups", "ent"), None), P(("groups", "ent"), None)),
        check_vma=False,
    )
```

```python
import functools

import jax
import jax.numpy as jnp
from jax import lax
from jax.experimental import pallas as pl
from jax.experimental.pallas import tpu as pltpu
from jax.sharding import PartitionSpec as P

BLK = 32
SPAN = 16
AG_PIECES = 4
RS_PIECES = 3
W = 256

temper = 2.0
learn_rate = 0.1
epsilon = 1e-10

F32 = jnp.float32
BF16 = jnp.bfloat16


def pieces(rows, count):
    tiles = rows // 16
    ends = [16 * (tiles * i // count) for i in range(count + 1)]
    return tuple((at, end - at) for at, end in zip(ends[:-1], ends[1:]))


def dot(a, b):
    return jnp.dot(a, b, preferred_element_type=F32)


def iota(shape, dim):
    return lax.broadcasted_iota(jnp.int32, shape, dim).astype(F32)


def onehot(mask):
    return jnp.where(mask, 1.0, 0.0).astype(BF16)


def sigmoid(x):
    return 1.0 / (1.0 + jnp.exp(-x))


def kernel(
    n,
    snake,
    table_hbm,
    edges,
    negative,
    block_map,
    rel_hbm,
    out,
    table,
    ag,
    agp,
    nid,
    nidp,
    rs,
    gath,
    rel,
    relg,
    ids_own,
    ids_part,
    idcol,
    grads,
    grads_part,
    negrow,
    negcol,
    negpart,
    negsend,
    negrecv,
    part,
    partneg,
    ag_send,
    ag_recv,
    agp_send,
    agp_recv,
    nid_send,
    nid_recv,
    nidp_send,
    nidp_recv,
    rs_send,
    rs_recv,
    x_send,
    x_recv,
    rel_sem,
    table_sem,
):
    feat, rows = table_hbm.shape
    dims = feat // 2
    edge_count = edges.shape[1]
    echunks = edge_count // W
    gchunks = 2 * echunks
    nneg = 2 * n * SPAN
    nchunks = nneg // W
    nblk = block_map.shape[1]
    rel_count = rel_hbm.shape[1]
    ag_rows = feat
    rs_rows = feat + 32
    ag_subs = pieces(ag_rows, AG_PIECES)
    rs_subs = pieces(rs_rows, RS_PIECES)

    me = lax.axis_index("ent")
    core = lax.rem(me, 2)
    chip = me // 2
    if snake:
        z, y = chip // 2, lax.rem(chip, 2)
        pos = (1 - y) * z + y * (n - 1 - z)
    else:
        pos = chip

    def chip_at(p):
        p = lax.rem(p + 2 * n, n)
        if not snake:
            return p
        f = p // (n // 2)
        return (1 - f) * 2 * p + f * (2 * (n - 1 - p) + 1)

    partner = 2 * chip + 1 - core
    nxt = (2 * chip_at(pos + 1) + core, 2 * chip_at(pos - 1) + core)

    halves = [slice(d * W, (d + 1) * W) for d in range(2)]
    table_copies = [
        pltpu.make_async_copy(table_hbm.at[:, cols], table.at[:, cols], table_sem.at[d])
        for d, cols in enumerate(halves)
    ]
    for copy in table_copies:
        copy.start()
    rel_copy = pltpu.make_async_copy(rel_hbm, rel, rel_sem)
    rel_copy.start()

    barrier = pltpu.get_barrier_semaphore()
    for other in (nxt[0], nxt[1], partner):
        pl.semaphore_signal(
            barrier, inc=1, device_id={"ent": other}, device_id_type=pl.DeviceIdType.MESH
        )

    def remote(src, dst, send, recv, to):
        return pltpu.make_async_remote_copy(
            src_ref=src,
            dst_ref=dst,
            send_sem=send,
            recv_sem=recv,
            device_id={"ent": to},
            device_id_type=pl.DeviceIdType.MESH,
        )

    def ag_copy(k, d, s):
        at, size = ag_subs[s]
        return remote(
            ag.at[k - 1, d, pl.ds(at, size)],
            ag.at[k, d, pl.ds(at, size)],
            ag_send.at[k, d, s],
            ag_recv.at[k, d, s],
            nxt[d],
        )

    def agp_copy(k, d):
        return remote(
            ag.at[k, d, pl.ds(0, ag_rows)],
            agp.at[k, d],
            agp_send.at[k, d],
            agp_recv.at[k, d],
            partner,
        )

    def nid_copy(k, d):
        return remote(
            nid.at[k - 1, d], nid.at[k, d], nid_send.at[k, d], nid_recv.at[k, d], nxt[d]
        )

    def nidp_copy(k, d):
        return remote(
            nid.at[k, d], nidp.at[k, d], nidp_send.at[k, d], nidp_recv.at[k, d], partner
        )

    def rs_copy(k, d, s):
        at, size = rs_subs[s]
        return remote(
            ag.at[k, d, pl.ds(at, size)],
            rs.at[k, d, pl.ds(at, size)],
            rs_send.at[k, d, s],
            rs_recv.at[k, d, s],
            nxt[d],
        )

    for d in range(2):
        table_copies[d].wait()
        ag[0, d, 0:feat, :] = table[:, d * W : (d + 1) * W].astype(BF16)
        nid[0, d] = jnp.full((1, 128), negative[0], jnp.int32).astype(F32)
    pl.semaphore_wait(barrier, 3)
    for d in range(2):
        nid_copy(1, d).start()
    for s in range(AG_PIECES):
        for d in range(2):
            ag_copy(1, d, s).start()
    for d in range(2):
        nidp_copy(0, d).start()
        agp_copy(0, d).start()

    ends = jnp.concatenate([edges[0:1, :], edges[2:3, :]], axis=1)
    mapped = block_map[...]
    parts = jnp.concatenate(
        [
            jnp.broadcast_to((mapped >> 5).astype(F32), (8, nblk)),
            jnp.broadcast_to((mapped & 31).astype(F32), (8, nblk)),
        ],
        axis=0,
    ).astype(BF16)
    for c in range(gchunks):
        cols = slice(c * W, (c + 1) * W)
        of = ends[:, cols]
        found = dot(parts, onehot(iota((nblk, W), 0) == (of >> 5).astype(F32)))
        ids_own[:, cols] = (found[0:8] * 32.0 + found[8:16]) * float(BLK) + (of & 31).astype(F32)
    ids_copy = remote(ids_own, ids_part, x_send.at[0], x_recv.at[0], partner)
    ids_copy.start()

    sub_iota = iota((W, W), 0)
    lane_iota = iota((1, W), 1)

    def set_columns(held, first):
        for c in range(gchunks):
            turned = jnp.transpose(held[:, c * W : (c + 1) * W])
            idcol[first + c] = jnp.broadcast_to(turned[:, 0:1], (W, 128))

    set_columns(ids_own, 0)

    rel_copy.wait()
    relg[...] = jnp.zeros_like(relg)

    @pl.loop(0, rel_count // W)
    def _(kk):
        cols = pl.ds(pl.multiple_of(kk * W, W), W)
        for c in range(echunks):
            local = edges[1:2, c * W : (c + 1) * W].astype(F32) - (kk * W).astype(F32)
            relg[c] += dot(rel[:, cols], onehot(sub_iota == local))

    gath[...] = jnp.zeros_like(gath)
    negpart[...] = jnp.zeros_like(negpart)
    ids_copy.wait()
    set_columns(ids_part, gchunks)

    def take(buf, spans, k, on_core, dirs=(0, 1)):
        for d in dirs:
            at_chip = chip_at(pos - k if d == 0 else pos + k)
            base = ((2 * at_chip + on_core) * rows + d * W).astype(F32)
            first = (on_core * (n * SPAN) + at_chip * SPAN).astype(F32)
            value = jnp.concatenate([spans[k, d]] * (W // 128), axis=1)
            slab = buf.at[k, d, pl.ds(0, feat)]
            for c in range(gchunks):
                local = ids_own[0:1, c * W : (c + 1) * W] - base
                gath[c] += dot(slab[...], onehot(sub_iota == local))
            for c in range(nchunks):
                place = lane_iota + (float(c * W) - first)
                local = jnp.where(
                    (place >= 0.0) & (place < float(SPAN)),
                    value * float(SPAN) + place - float(d * W),
                    -1.0,
                )
                gath[gchunks + c] += dot(slab[...], onehot(sub_iota == local))

    take(ag, nid, 0, core)

    @pl.loop(1, n)
    def _(k):
        for d in range(2):
            nid_copy(k, d).wait_recv()

            @pl.when(k < n - 1)
            def _():
                nid_copy(k + 1, d).start()

            nidp_copy(k, d).start()
        for s in range(AG_PIECES):
            for d in range(2):
                ag_copy(k, d, s).wait_recv()

                @pl.when(k < n - 1)
                def _():
                    ag_copy(k + 1, d, s).start()

            if s < 2:
                nidp_copy(k - 1, s).wait_recv()
                agp_copy(k - 1, s).wait_recv()
                take(agp, nidp, k - 1, 1 - core, (s,))
        for d in range(2):
            agp_copy(k, d).start()
        take(ag, nid, k, core)

    for d in range(2):
        nidp_copy(n - 1, d).wait_recv()
        agp_copy(n - 1, d).wait_recv()
    take(agp, nidp, n - 1, 1 - core)

    @pl.loop(0, n)
    def _(k):
        for d in range(2):
            agp_copy(k, d).wait_send()
            nidp_copy(k, d).wait_send()

            @pl.when(k > 0)
            def _():
                nid_copy(k, d).wait_send()
                for s in range(AG_PIECES):
                    ag_copy(k, d, s).wait_send()

    def grads_copy(c):
        return remote(grads.at[c], grads_part.at[c], x_send.at[2 + c], x_recv.at[2 + c], partner)

    for c in range(nchunks):
        held = gath[gchunks + c]
        negcol[:, c * W : (c + 1) * W] = held.astype(BF16)
        negrow[c * W : (c + 1) * W, :] = jnp.transpose(held).astype(BF16)
    for c in range(echunks):
        head, tail, rl = gath[c], gath[echunks + c], relg[c]
        h_re, h_im, r_re, r_im = head[:dims], head[dims:], rl[:dims], rl[dims:]
        queries = jnp.concatenate([h_re * r_re - h_im * r_im, h_re * r_im + h_im * r_re], axis=0)
        queries_bf = queries.astype(BF16)
        positive = jnp.sum(queries * tail, axis=0, keepdims=True)
        score = dot(negrow[...], queries_bf)
        tempered = jnp.exp(temper * score)
        weights = tempered / jnp.sum(tempered, axis=0, keepdims=True)
        grad_positive = -(1.0 - sigmoid(positive))
        grad_negative = (weights * sigmoid(score)).astype(BF16)
        grad_query = grad_positive * tail + dot(negcol[...], grad_negative)
        g_re, g_im = grad_query[:dims], grad_query[dims:]
        grads[c] = jnp.concatenate(
            [g_re * r_re + g_im * r_im, g_im * r_re - g_re * r_im], axis=0
        ).astype(BF16)
        grads[echunks + c] = (grad_positive * queries).astype(BF16)
        grads_copy(c).start()
        grads_copy(echunks + c).start()
        negpart[:, 0:feat] += lax.dot_general(
            grad_negative, queries_bf, (((1,), (1,)), ((), ())), preferred_element_type=F32
        )
    half = n * SPAN
    negsend[...] = negpart[pl.ds(pl.multiple_of((1 - core) * half, half), half), :].astype(BF16)
    neg_copy = remote(negsend, negrecv, x_send.at[1], x_recv.at[1], partner)
    neg_copy.start()

    lanes = iota((W, 128), 1)

    def gradient_part(k, d, held, first, fresh):
        at_chip = chip_at(pos - 1 - k if d == 0 else pos + 1 + k)
        base = ((2 * at_chip + core) * rows + d * W).astype(F32)
        total = None
        for c in range(gchunks):
            col = idcol[first + c] - base
            mask = jnp.concatenate([onehot(col == lanes), onehot(col == lanes + 128.0)], axis=1)
            one = dot(held[c], mask)
            total = one if total is None else total + one
        if fresh:
            part[d] = total
        else:
            part[d] += total

    def negative_part(k, d):
        at_chip = chip_at(pos - 1 - k if d == 0 else pos + 1 + k)
        own = negpart[pl.ds(pl.multiple_of(core * half + at_chip * SPAN, SPAN), SPAN), d * W : (d + 1) * W]
        other = negrecv[pl.ds(pl.multiple_of(at_chip * SPAN, SPAN), SPAN), d * W : (d + 1) * W]
        partneg[d] = own + other.astype(F32)

    def send_out(k, d, s, arrived):
        at, size = rs_subs[s]
        end = min(at + size, feat)
        value = part[d, at:end]
        if arrived:
            value = value + rs[k - 1, d, at:end].astype(F32)
        ag[k, d, at:end] = value.astype(BF16)
        if at + size > feat:
            neg = partneg[d]
            if arrived:
                neg = neg + (
                    rs[k - 1, d, feat : feat + 16].astype(F32)
                    + rs[k - 1, d, feat + 16 : feat + 32].astype(F32)
                )
            high = neg.astype(BF16)
            ag[k, d, feat : feat + 16] = high
            ag[k, d, feat + 16 : feat + 32] = (neg - high.astype(F32)).astype(BF16)
        rs_copy(k, d, s).start()

    for d in range(2):
        gradient_part(0, d, grads, 0, True)
    for c in range(gchunks):
        grads_copy(c).wait()
    for d in range(2):
        gradient_part(0, d, grads_part, gchunks, False)
    neg_copy.wait()
    for d in range(2):
        negative_part(0, d)
    for s in range(RS_PIECES):
        for d in range(2):
            send_out(0, d, s, False)

    def both(k):
        for d in range(2):
            gradient_part(k, d, grads, 0, True)
            gradient_part(k, d, grads_part, gchunks, False)
            negative_part(k, d)

    @pl.loop(1, n - 1)
    def _(k):
        both(k)
        for s in range(RS_PIECES):
            for d in range(2):
                rs_copy(k - 1, d, s).wait_recv()
                send_out(k, d, s, True)

    both(n - 1)
    last = n - 2
    spot = jnp.full((1, rows), negative[0], jnp.int32).astype(F32) * float(SPAN)
    span_iota = iota((SPAN, rows), 0)
    row_iota = iota((1, rows), 1)
    mask = jnp.where(row_iota - spot == span_iota, 1.0, 0.0)
    mask = jnp.concatenate([mask, mask], axis=0).astype(BF16)
    for d in range(2):
        for s in range(RS_PIECES):
            rs_copy(last, d, s).wait_recv()
        out[:, d * W : (d + 1) * W] = part[d] + rs[last, d, 0:feat].astype(F32)
    for d in range(2):
        neg = partneg[d] + (
            rs[last, d, feat : feat + 16].astype(F32) + rs[last, d, feat + 16 : feat + 32].astype(F32)
        )
        high = neg.astype(BF16).astype(F32)
        pair = jnp.concatenate([high, neg - high], axis=0).astype(BF16)
        spread = lax.dot_general(
            pair, mask, (((0,), (0,)), ((), ())), preferred_element_type=F32
        )
        size = min(feat - d * W, W)
        out[d * W : d * W + size, :] += spread[:size]

    @pl.loop(0, n - 1)
    def _(k):
        for d in range(2):
            for s in range(RS_PIECES):
                rs_copy(k, d, s).wait_send()


def gradient_of(table, edges, negatives, block_map, relations, n):
    feat, rows = table.shape
    edge_count = edges.shape[1]
    gchunks = 2 * edge_count // W
    nneg = 2 * n * SPAN
    dma = pltpu.SemaphoreType.DMA
    vmem = pl.BlockSpec(memory_space=pltpu.VMEM)
    return pl.pallas_call(
        functools.partial(kernel, n, n == 8),
        out_shape=jax.ShapeDtypeStruct((feat, rows), F32),
        in_specs=[
            pl.BlockSpec(memory_space=pl.ANY),
            vmem,
            pl.BlockSpec(memory_space=pltpu.SMEM),
            vmem,
            pl.BlockSpec(memory_space=pl.ANY),
        ],
        out_specs=vmem,
        scratch_shapes=[
            pltpu.VMEM((feat, rows), F32),
            pltpu.VMEM((n, 2, feat + 32, W), BF16),
            pltpu.VMEM((n, 2, feat, W), BF16),
            pltpu.VMEM((n, 2, 1, 128), F32),
            pltpu.VMEM((n, 2, 1, 128), F32),
            pltpu.VMEM((n - 1, 2, feat + 32, W), BF16),
            pltpu.VMEM((gchunks + nneg // W, feat, W), F32),
            pltpu.VMEM(relations.shape, BF16),
            pltpu.VMEM((edge_count // W, feat, W), F32),
            pltpu.VMEM((8, 2 * edge_count), F32),
            pltpu.VMEM((8, 2 * edge_count), F32),
            pltpu.VMEM((2 * gchunks, W, 128), F32),
            pltpu.VMEM((gchunks, feat, W), BF16),
            pltpu.VMEM((gchunks, feat, W), BF16),
            pltpu.VMEM((nneg, feat), BF16),
            pltpu.VMEM((feat, nneg), BF16),
            pltpu.VMEM((nneg, 2 * W), F32),
            pltpu.VMEM((nneg // 2, 2 * W), BF16),
            pltpu.VMEM((nneg // 2, 2 * W), BF16),
            pltpu.VMEM((2, feat, W), F32),
            pltpu.VMEM((2, SPAN, W), F32),
            dma((n, 2, AG_PIECES)),
            dma((n, 2, AG_PIECES)),
            dma((n, 2)),
            dma((n, 2)),
            dma((n, 2)),
            dma((n, 2)),
            dma((n, 2)),
            dma((n, 2)),
            dma((n - 1, 2, RS_PIECES)),
            dma((n - 1, 2, RS_PIECES)),
            dma((2 + gchunks,)),
            dma((2 + gchunks,)),
            dma,
            dma((2,)),
        ],
        compiler_params=pltpu.CompilerParams(
            collective_id=0, has_side_effects=True, vmem_limit_bytes=60 * 2**20
        ),
        name="complex_step",
    )(table, edges, negatives, block_map, relations)


def update_kernel(table, accum, gradient, new_table, new_accum):
    grad = gradient[...]
    total = accum[...] + grad * grad
    new_accum[...] = total
    new_table[...] = table[...] - learn_rate * grad / (jnp.sqrt(total) + epsilon)


def updated(table, accum, gradient):
    feat, rows = table.shape
    block = pl.BlockSpec((feat // 2, rows), lambda i: (i, 0))
    whole = jax.ShapeDtypeStruct((feat, rows), F32)
    return pl.pallas_call(
        update_kernel,
        out_shape=(whole, whole),
        grid=(2,),
        in_specs=[block] * 3,
        out_specs=(block, block),
        compiler_params=pltpu.CompilerParams(vmem_limit_bytes=16 * 2**20),
        name="adagrad",
    )(table, accum, gradient)


def on_device(table, accum, relations, edges, negatives, block_map):
    n = lax.axis_size("ent") // 2
    gradient = gradient_of(table.T, edges.T, negatives, block_map.reshape(1, -1), relations.T, n)
    new_table, new_accum = updated(table.T, accum.T, gradient)
    return (new_table.T, new_accum.T)


def solution(mesh):
    placed = (
        P(("groups", "ent"), None),
        P(("groups", "ent"), None),
        P("groups", None),
        P(("groups", "ent"), None),
        P(("groups", "ent")),
        P("groups"),
    )
    return jax.shard_map(
        on_device,
        mesh=mesh,
        in_specs=placed,
        out_specs=(P(("groups", "ent"), None), P(("groups", "ent"), None)),
        check_vma=False,
    )
```
